32 devices in a mesh: groups: 2 (over y), dp: 16 (over z, x, core).
Axes of the slice: x: 2, y: 2, z: 4, core: 2. Of those that a mesh axis runs over, the one named last changes fastest.
Arguments:
- query_grads: bfloat16 [128, 8192], P('dp'), may hold values from -6 to 6
- train_factors: bfloat16 [32, 128, 512], P(('groups', 'dp')), parts along dimension 0, may hold values from -6 to 6
- lengths: int32 [32], P(('groups', 'dp')), parts along dimension 0, may hold values from 1 to 128, as said below
- owner: int32 [32], P('groups'), parts along dimension 0, may hold values from 0 to 15, each once
- basis_in: bfloat16 [8, 32, 32], replicated, may hold values from -1 to 1
- basis_out: bfloat16 [8, 32, 32], replicated, may hold values from -1 to 1
- eigenvalues: float32 [8, 32, 32], replicated, may hold values from 0.01 to 10
Outputs:
- scores: float32 [32, 128], P(('groups', 'dp')), parts along dimension 0
The draws below stay inside these ranges and needn't reach their ends.
There are 2 independent parts, one for each index of `groups`. The reference program is written for one: setup_inputs(seed, part) draws one part's arguments, and reference() takes and returns one part's arrays. A program takes and returns all parts, laid end to end along the dimension named above; an argument that names none is the same for every part. Nothing has to cross between parts.
Inputs may be any that keep to these rules, and one draw needn't show every extreme that they name: `lengths`: every training sequence has at least one live token; in every draw some sequence is fully live. owner is a permutation of the training sequences.
All inputs are finite; a program needn't handle non-finite values.
Results may differ from the reference program's by a relative error of at most 0.0042.
Values may be sent and summed in bfloat16 or wider, within the bound.
A program may use at most 64 MiB of HBM per device.

```python
import math
import jax
import jax.numpy as jnp
from jax import lax

LAYERS = 8
RANK = 32
TOK = 128
SEQS = 16
QUERIES = 128


def draw_lengths(key, part):
    key = jax.random.fold_in(key, 11)
    first, second = jax.random.split(key)
    values = jax.random.randint(first, (SEQS,), 1, TOK + 1)
    spot = jax.random.randint(second, (), 0, SEQS)
    return jnp.where(jnp.arange(SEQS) == spot, TOK, values).astype(jnp.int32)


def levels(own_key, dims, pieces, smallest, largest):
    factor_of, own = 1.0, jax.random.fold_in(own_key, 6)
    for axis_at, shards_of in pieces:
        draws = jnp.exp(jax.random.uniform(jax.random.fold_in(own, axis_at), (shards_of,), jnp.float32, smallest / len(pieces), largest / len(pieces)))
        factor_of = factor_of * jnp.repeat(draws, dims[axis_at] // shards_of).reshape([-1 if axis == axis_at else 1 for axis in range(len(dims))])
    return factor_of


def scatter_about(stream_key, dims, spread, most, pieces=(), held_as=jnp.bfloat16):
    array = jax.random.normal(stream_key, dims, jnp.float32) * spread
    if len(pieces) > 0:
        array = levels(stream_key, dims, pieces, -0.22, 0.18) * array
    return jnp.clip(array, min=-most, max=most).astype(held_as)


def setup_inputs(seed: int = 0, part: int = 0) -> dict:
    splits = jax.random.split(jax.random.key(seed), 8)
    part_keys = jax.random.split(jax.random.fold_in(splits[7], part), 8)
    return {
        "query_grads": scatter_about(splits[0], (QUERIES, LAYERS * RANK * RANK), 1.0, 6.0, ((0, 16),)),
        "train_factors": scatter_about(part_keys[1], (SEQS, TOK, 2 * LAYERS * RANK), 1.0, 6.0, ((0, 16),)),
        "lengths": draw_lengths(jax.random.fold_in(jax.random.fold_in(splits[7], part), 71), part),
        "owner": jax.random.permutation(part_keys[3], SEQS).astype(jnp.int32),
        "basis_in": scatter_about(splits[4], (LAYERS, RANK, RANK), RANK ** -0.5, 1.0),
        "basis_out": scatter_about(splits[5], (LAYERS, RANK, RANK), RANK ** -0.5, 1.0),
        "eigenvalues": jnp.clip(jnp.exp(jax.random.uniform(splits[6], (LAYERS, RANK, RANK), jnp.float32, math.log(0.01), math.log(10.0))), 0.01, 10.0),
    }


def precondition(query_grads, basis_in, basis_out, eigenvalues):
    layers, rank = (eigenvalues.shape[0], eigenvalues.shape[1])
    grads = query_grads.reshape(query_grads.shape[0], layers, rank, rank).astype(jnp.float32)
    half = jnp.einsum('qlij,ljk->qlik', grads, basis_in.astype(jnp.float32)).astype(jnp.bfloat16)
    rotated = jnp.einsum('lio,qlik->qlok', basis_out.astype(jnp.float32), half.astype(jnp.float32))
    damp = 0.1 * lax.optimization_barrier(jnp.mean(eigenvalues, axis=(1, 2), keepdims=True))
    scaled = rotated / (eigenvalues + damp)[None]
    return scaled.astype(jnp.bfloat16).reshape(query_grads.shape[0], layers * rank * rank)

def reference(query_grads, train_factors, lengths, owner, basis_in, basis_out, eigenvalues):
    layers, rank = (eigenvalues.shape[0], eigenvalues.shape[1])
    seqs, tokens = (train_factors.shape[0], train_factors.shape[1])
    precond = precondition(query_grads, basis_in, basis_out, eigenvalues)
    rows = train_factors.reshape(seqs * tokens, 2, layers, rank).astype(jnp.float32)
    rot_in = jnp.einsum('nlj,ljk->nlk', rows[:, 0], basis_in.astype(jnp.float32)).astype(jnp.bfloat16)
    rot_out = jnp.einsum('nli,lio->nlo', rows[:, 1], basis_out.astype(jnp.float32)).astype(jnp.bfloat16)
    rot_in = rot_in.reshape(seqs, tokens, layers, rank).astype(jnp.float32)
    rot_out = rot_out.reshape(seqs, tokens, layers, rank).astype(jnp.float32)
    positions = lax.broadcasted_iota(jnp.int32, (seqs, tokens), 1)
    mask = (positions < lengths[:, None]).astype(jnp.float32)
    gram = jnp.einsum('stlo,stlk->slok', rot_out * mask[:, :, None, None], rot_in)
    gram = gram.reshape(seqs, layers * rank * rank)
    scale = 1.0 / (rank * math.sqrt(tokens))
    influence = jnp.dot(gram, precond.astype(jnp.float32).T, precision=lax.Precision.HIGHEST) * scale
    return influence[owner]
```

```python
import functools
import math

import jax
import jax.numpy as jnp
from jax import lax
from jax.experimental import pallas as pl
from jax.experimental.pallas import tpu as pltpu
from jax.sharding import PartitionSpec as P

LANES = 128
SUB = 8
NT = (((1,), (1,)), ((), ()))


def nt_dot(a, b, **kw):
    return lax.dot_general(a, b, NT, preferred_element_type=jnp.float32, **kw)


def nn_dot(a, b, **kw):
    return jnp.dot(a, b, preferred_element_type=jnp.float32, **kw)


def iota(shape, dim):
    return lax.broadcasted_iota(jnp.int32, shape, dim)


def each(count, body):
    if count <= 16:
        for step in range(count):
            body(step)
    else:
        lax.fori_loop(0, count, lambda step, c: (body(step), c)[1], 0)


def kernel(n, parts, layers, rank, tokens, q_dev,
           len_ref, own_ref, grads_hbm, fact_hbm, bin_hbm, bout_hbm, eig_hbm,
           out_ref,
           fact, b_in, b_out, eig, bo32, gbuf, hsend, hbuf, score, ssend, sbuf,
           load_sem, gself_sem, gsend_sem, grecv_sem,
           hsend_sem, hrecv_sem, ssend_sem, srecv_sem):
    me = lax.axis_index("dp")
    group = me // parts
    part = me % parts
    width = layers * rank
    feats = layers * rank * rank
    share = feats // parts
    chunks = share // LANES
    per = LANES // rank

    loads = [
        pltpu.make_async_copy(src, dst, load_sem.at[i])
        for i, (src, dst) in enumerate(
            [(bin_hbm, b_in), (bout_hbm, b_out), (eig_hbm, eig), (fact_hbm, fact)]
        )
    ]
    for load in loads:
        load.start()
    own_grads = pltpu.make_async_copy(
        grads_hbm.at[:, pl.ds(pl.multiple_of(part * share, share), share)],
        gbuf.at[part], gself_sem)
    own_grads.start()

    barrier = pltpu.get_barrier_semaphore()

    def greet(step):
        peer = (me + step + 1) % n
        pl.semaphore_signal(barrier, inc=1, device_id={"dp": peer},
                            device_id_type=pl.DeviceIdType.MESH)

    each(n - 1, greet)
    pl.semaphore_wait(barrier, n - 1)

    def send_grads(step):
        other = (part + step + 1) % parts
        pltpu.make_async_remote_copy(
            grads_hbm.at[:, pl.ds(pl.multiple_of(other * share, share), share)],
            gbuf.at[part], gsend_sem, grecv_sem,
            device_id={"dp": group * parts + other},
            device_id_type=pl.DeviceIdType.MESH).start()

    each(parts - 1, send_grads)

    for load in loads[:3]:
        load.wait()
    bi = b_in[...].reshape(width, rank)
    bo = b_out[...].reshape(width, rank)
    spread = (iota((rank, width), 0) == iota((rank, width), 1) % rank).astype(jnp.bfloat16)
    spread_t = (iota((width, rank), 0) % rank == iota((width, rank), 1)).astype(jnp.bfloat16)
    lane_layer = iota((width, width), 1) // rank
    same = iota((width, width), 0) // rank == lane_layer
    diag_in32 = jnp.where(same, nn_dot(bi, spread), 0.0)
    diag_in = diag_in32.astype(jnp.bfloat16)
    diag_out_t = jnp.where(same, nt_dot(spread_t, bo), 0.0).astype(jnp.bfloat16)
    rows_in = jnp.sum(diag_in32.reshape(layers, rank, width), axis=0)
    rows_in = jnp.concatenate([rows_in] * per, axis=0).astype(jnp.bfloat16)
    bo32[...] = bo.astype(jnp.float32)
    shuffled = jnp.concatenate(
        [bo32[pl.ds(low, width // per, stride=per), :] for low in range(per)], axis=0
    ).astype(jnp.bfloat16)
    in_order = (iota((width, width), 0) % (width // per)) // (rank // per) == lane_layer
    diag_out = jnp.where(in_order, nn_dot(shuffled, spread), 0.0).astype(jnp.bfloat16)
    values = eig[...]
    damp = 0.1 * (jnp.sum(values, axis=(1, 2), keepdims=True) * (1.0 / (rank * rank)))
    weight = (1.0 / (values + damp)).reshape(width, rank)
    weight = nn_dot(weight, spread.astype(jnp.float32), precision=lax.Precision.HIGHEST)
    weight = jnp.where(same, weight, 0.0)

    loads[3].wait()
    rot_in = nn_dot(fact[0, :, :width], diag_in).astype(jnp.bfloat16)
    rot_out = nt_dot(diag_out_t, fact[0, :, width:])
    live = iota((width, tokens), 1) < len_ref[0]
    rot_out = jnp.where(live, rot_out, 0.0).astype(jnp.bfloat16)
    gram = nn_dot(rot_out, rot_in)
    scaled = (gram * weight).astype(jnp.bfloat16)
    back = nt_dot(scaled, rows_in).astype(jnp.bfloat16)
    back = nn_dot(diag_out, back)
    rows = width // per
    slot = iota((rows, LANES), 1) // rank
    total = jnp.zeros((rows, LANES), jnp.float32)
    for low in range(per):
        total = jnp.where(slot == low, back[low * rows:(low + 1) * rows], total)
    hsend[...] = total

    def part_rows(which):
        return pl.ds(pl.multiple_of(which * chunks, chunks), chunks)

    def send_rows(step):
        peer = (me + step + 1) % n
        pltpu.make_async_remote_copy(
            hsend.at[part_rows(peer % parts)], hbuf.at[part_rows(me)],
            hsend_sem, hrecv_sem, device_id={"dp": peer},
            device_id_type=pl.DeviceIdType.MESH).start()

    each(n - 1, send_rows)
    hbuf[part_rows(me), :] = hsend[part_rows(part), :]

    own_grads.wait()
    some = gbuf.at[pl.ds(0, parts - 1)]
    pltpu.make_async_copy(some, some, grecv_sem).wait()
    grads = gbuf[...].astype(jnp.float32).reshape(parts * q_dev, share).astype(jnp.bfloat16)
    grads = jnp.concatenate([grads] * (LANES // (parts * q_dev)), axis=0)
    others = hbuf.at[pl.ds(0, (n - 1) * chunks)]
    pltpu.make_async_copy(others, others, hrecv_sem).wait()
    sums = jnp.concatenate(
        [hbuf[pl.ds(c, n, stride=chunks), :].astype(jnp.bfloat16) for c in range(chunks)], axis=1)
    score[...] = nt_dot(sums, grads)

    def order(step):
        ssend[step] = score[pl.ds(own_ref[step], 1), :]

    each(n, order)

    def send_score(step):
        peer = (me + step + 1) % n
        pltpu.make_async_remote_copy(
            ssend.at[peer], sbuf.at[me], ssend_sem, srecv_sem, device_id={"dp": peer},
            device_id_type=pl.DeviceIdType.MESH).start()

    each(n - 1, send_score)
    sbuf[me] = ssend[me]
    rest = sbuf.at[pl.ds(0, n - 1)]
    pltpu.make_async_copy(rest, rest, srecv_sem).wait()

    scale = 1.0 / (rank * math.sqrt(tokens))
    span = parts * q_dev
    lane = iota((1, LANES), 1) // span
    per_block = LANES // span
    for block in range(n // parts // per_block):
        row = jnp.zeros((1, LANES), jnp.float32)
        for at in range(per_block):
            low = (block * per_block + at) * parts
            row = jnp.where(lane == at, jnp.sum(sbuf[low:low + parts], axis=0), row)
        out_ref[:, block * LANES:(block + 1) * LANES] = row * scale

    pltpu.make_async_copy(some, some, gsend_sem).wait()
    pltpu.make_async_copy(others, others, hsend_sem).wait()
    pltpu.make_async_copy(rest, rest, ssend_sem).wait()


def local(query_grads, train_factors, lengths, owner, basis_in, basis_out, eigenvalues):
    layers, rank = (eigenvalues.shape[0], eigenvalues.shape[1])
    n = lax.axis_size("dp")
    seqs, tokens, cols = train_factors.shape
    q_dev, feats = query_grads.shape
    parts = feats // (SUB * LANES)
    share = feats // parts
    width = layers * rank
    chunks = share // LANES
    hbm = pl.BlockSpec(memory_space=pl.ANY)
    smem = pl.BlockSpec(memory_space=pltpu.SMEM)
    dma = pltpu.SemaphoreType.DMA
    return pl.pallas_call(
        functools.partial(kernel, n, parts, layers, rank, tokens, q_dev),
        out_shape=jax.ShapeDtypeStruct((1, n * q_dev), jnp.float32),
        in_specs=[smem, smem, hbm, hbm, hbm, hbm, hbm],
        out_specs=pl.BlockSpec(memory_space=pltpu.VMEM),
        scratch_shapes=[
            pltpu.VMEM((seqs, tokens, cols), jnp.bfloat16),
            pltpu.VMEM((layers, rank, rank), jnp.bfloat16),
            pltpu.VMEM((layers, rank, rank), jnp.bfloat16),
            pltpu.VMEM((layers, rank, rank), jnp.float32),
            pltpu.VMEM((width, rank), jnp.float32),
            pltpu.VMEM((parts, q_dev, share), jnp.bfloat16),
            pltpu.VMEM((feats // LANES, LANES), jnp.float32),
            pltpu.VMEM((n * chunks, LANES), jnp.float32),
            pltpu.VMEM((n, LANES), jnp.float32),
            pltpu.VMEM((n, 1, LANES), jnp.float32),
            pltpu.VMEM((n, 1, LANES), jnp.float32),
            dma((4,)), dma, dma, dma, dma, dma, dma, dma,
        ],
        compiler_params=pltpu.CompilerParams(
            collective_id=0, has_side_effects=True, vmem_limit_bytes=32 * 1024 * 1024),
    )(lengths, owner, query_grads, train_factors, basis_in, basis_out, eigenvalues)


def solution(mesh):
    return jax.shard_map(
        local,
        mesh=mesh,
        in_specs=(
            P("dp", None),
            P(("groups", "dp"), None, None),
            P(("groups", "dp")),
            P("groups"),
            P(),
            P(),
            P(),
        ),
        out_specs=P(("groups", "dp"), None),
        check_vma=False,
    )
```

```python
import functools
import math

import jax
import jax.numpy as jnp
from jax import lax
from jax.experimental import pallas as pl
from jax.experimental.pallas import tpu as pltpu
from jax.sharding import PartitionSpec as P

LANES = 128
SUB = 8
NT = (((1,), (1,)), ((), ()))


def nt_dot(a, b, **kw):
    return lax.dot_general(a, b, NT, preferred_element_type=jnp.float32, **kw)


def nn_dot(a, b, **kw):
    return jnp.dot(a, b, preferred_element_type=jnp.float32, **kw)


def iota(shape, dim):
    return lax.broadcasted_iota(jnp.int32, shape, dim)


def each(count, body):
    if count <= 16:
        for step in range(count):
            body(step)
    else:
        lax.fori_loop(0, count, lambda step, c: (body(step), c)[1], 0)


def kernel(n, parts, layers, rank, tokens, q_dev,
           len_hbm, own_hbm, grads_hbm, fact_hbm, bin_hbm, bout_hbm, eig_hbm,
           out_ref,
           len_ref, own_ref, fact, b_in, b_out, eig, bo32, gbuf, hsend, hbuf, wide, score, ssend, sbuf,
           load_sem, gself_sem, gsend_sem, grecv_sem,
           hsend_sem, hrecv_sem, ssend_sem, srecv_sem):
    me = lax.axis_index("dp")
    group = me // parts
    part = me % parts
    width = layers * rank
    feats = layers * rank * rank
    share = feats // parts
    chunks = share // LANES
    per = LANES // rank

    loads = [
        pltpu.make_async_copy(src, dst, load_sem.at[i])
        for i, (src, dst) in enumerate(
            [(bin_hbm, b_in), (bout_hbm, b_out), (eig_hbm, eig), (fact_hbm, fact),
             (len_hbm, len_ref), (own_hbm, own_ref)]
        )
    ]
    for load in loads:
        load.start()
    own_grads = pltpu.make_async_copy(
        grads_hbm.at[:, pl.ds(pl.multiple_of(part * share, share), share)],
        gbuf.at[part], gself_sem)
    own_grads.start()

    barrier = pltpu.get_barrier_semaphore()

    def greet(step):
        peer = (me + step + 1) % n
        pl.semaphore_signal(barrier, inc=1, device_id={"dp": peer},
                            device_id_type=pl.DeviceIdType.MESH)

    each(n - 1, greet)
    pl.semaphore_wait(barrier, n - 1)

    def send_grads(step):
        other = (part + step + 1) % parts
        pltpu.make_async_remote_copy(
            grads_hbm.at[:, pl.ds(pl.multiple_of(other * share, share), share)],
            gbuf.at[part], gsend_sem, grecv_sem,
            device_id={"dp": group * parts + other},
            device_id_type=pl.DeviceIdType.MESH).start()

    each(parts - 1, send_grads)

    for load in loads[:3]:
        load.wait()
    bi = b_in[...].reshape(width, rank)
    bo = b_out[...].reshape(width, rank)
    spread = (iota((rank, width), 0) == iota((rank, width), 1) % rank).astype(jnp.bfloat16)
    spread_t = (iota((width, rank), 0) % rank == iota((width, rank), 1)).astype(jnp.bfloat16)
    lane_layer = iota((width, width), 1) // rank
    same = iota((width, width), 0) // rank == lane_layer
    diag_in32 = jnp.where(same, nn_dot(bi, spread), 0.0)
    diag_in = diag_in32.astype(jnp.bfloat16)
    diag_out_t = jnp.where(same, nt_dot(spread_t, bo), 0.0).astype(jnp.bfloat16)
    rows_in = jnp.sum(diag_in32.reshape(layers, rank, width), axis=0)
    rows_in = jnp.concatenate([rows_in] * per, axis=0).astype(jnp.bfloat16)
    bo32[...] = bo.astype(jnp.float32)
    shuffled = jnp.concatenate(
        [bo32[pl.ds(low, width // per, stride=per), :] for low in range(per)], axis=0
    ).astype(jnp.bfloat16)
    in_order = (iota((width, width), 0) % (width // per)) // (rank // per) == lane_layer
    diag_out = jnp.where(in_order, nn_dot(shuffled, spread), 0.0).astype(jnp.bfloat16)
    values = eig[...]
    damp = 0.1 * (jnp.sum(values, axis=(1, 2), keepdims=True) * (1.0 / (rank * rank)))
    weight = (1.0 / (values + damp)).reshape(width, rank)
    weight = nn_dot(weight, spread.astype(jnp.float32), precision=lax.Precision.HIGHEST)
    weight = jnp.where(same, weight, 0.0)

    for load in loads[3:]:
        load.wait()
    rot_in = nn_dot(fact[0, :, :width], diag_in).astype(jnp.bfloat16)
    rot_out = nt_dot(diag_out_t, fact[0, :, width:])
    live = iota((width, tokens), 1) < len_ref[0]
    rot_out = jnp.where(live, rot_out, 0.0).astype(jnp.bfloat16)
    gram = nn_dot(rot_out, rot_in)
    scaled = (gram * weight).astype(jnp.bfloat16)
    back = nt_dot(scaled, rows_in).astype(jnp.bfloat16)
    back = nn_dot(diag_out, back)
    rows = width // per
    slot = iota((rows, LANES), 1) // rank
    total = jnp.zeros((rows, LANES), jnp.float32)
    for low in range(per):
        total = jnp.where(slot == low, back[low * rows:(low + 1) * rows], total)
    hsend[...] = total.reshape(parts, chunks, LANES).astype(jnp.bfloat16)

    def send_rows(step):
        peer = (me + step + 1) % n
        pltpu.make_async_remote_copy(
            hsend.at[peer % parts], hbuf.at[me],
            hsend_sem, hrecv_sem, device_id={"dp": peer},
            device_id_type=pl.DeviceIdType.MESH).start()

    each(n - 1, send_rows)
    hbuf[me] = hsend[part]

    own_grads.wait()
    some = gbuf.at[pl.ds(0, parts - 1)]
    pltpu.make_async_copy(some, some, grecv_sem).wait()
    grads = gbuf[...].astype(jnp.float32).reshape(parts * q_dev, share).astype(jnp.bfloat16)
    grads = jnp.concatenate([grads] * (LANES // (parts * q_dev)), axis=0)
    others = hbuf.at[pl.ds(0, n - 1)]
    pltpu.make_async_copy(others, others, hrecv_sem).wait()
    wide[...] = hbuf[...].astype(jnp.float32).reshape(n * chunks, LANES)
    sums = jnp.concatenate(
        [wide[pl.ds(c, n, stride=chunks), :].astype(jnp.bfloat16) for c in range(chunks)], axis=1)
    score[...] = nt_dot(sums, grads)

    def order(step):
        ssend[step] = score[pl.ds(own_ref[step], 1), :]

    each(n, order)

    def send_score(step):
        peer = (me + step + 1) % n
        pltpu.make_async_remote_copy(
            ssend.at[peer], sbuf.at[me], ssend_sem, srecv_sem, device_id={"dp": peer},
            device_id_type=pl.DeviceIdType.MESH).start()

    each(n - 1, send_score)
    sbuf[me] = ssend[me]
    rest = sbuf.at[pl.ds(0, n - 1)]
    pltpu.make_async_copy(rest, rest, srecv_sem).wait()

    scale = 1.0 / (rank * math.sqrt(tokens))
    span = parts * q_dev
    lane = iota((1, LANES), 1) // span
    per_block = LANES // span
    for block in range(n // parts // per_block):
        row = jnp.zeros((1, LANES), jnp.float32)
        for at in range(per_block):
            low = (block * per_block + at) * parts
            row = jnp.where(lane == at, jnp.sum(sbuf[low:low + parts], axis=0), row)
        out_ref[:, block * LANES:(block + 1) * LANES] = row * scale

    pltpu.make_async_copy(some, some, gsend_sem).wait()
    pltpu.make_async_copy(others, others, hsend_sem).wait()
    pltpu.make_async_copy(rest, rest, ssend_sem).wait()


def local(query_grads, train_factors, lengths, owner, basis_in, basis_out, eigenvalues):
    layers, rank = (eigenvalues.shape[0], eigenvalues.shape[1])
    n = lax.axis_size("dp")
    seqs, tokens, cols = train_factors.shape
    q_dev, feats = query_grads.shape
    parts = feats // (SUB * LANES)
    share = feats // parts
    width = layers * rank
    chunks = share // LANES
    hbm = pl.BlockSpec(memory_space=pltpu.HBM)
    dma = pltpu.SemaphoreType.DMA
    return pl.pallas_call(
        functools.partial(kernel, n, parts, layers, rank, tokens, q_dev),
        out_shape=jax.ShapeDtypeStruct((1, n * q_dev), jnp.float32),
        in_specs=[hbm] * 7,
        out_specs=pl.BlockSpec(memory_space=pltpu.VMEM),
        scratch_shapes=[
            pltpu.SMEM(lengths.shape, jnp.int32),
            pltpu.SMEM(owner.shape, jnp.int32),
            pltpu.VMEM((seqs, tokens, cols), jnp.bfloat16),
            pltpu.VMEM((layers, rank, rank), jnp.bfloat16),
            pltpu.VMEM((layers, rank, rank), jnp.bfloat16),
            pltpu.VMEM((layers, rank, rank), jnp.float32),
            pltpu.VMEM((width, rank), jnp.float32),
            pltpu.VMEM((parts, q_dev, share), jnp.bfloat16),
            pltpu.VMEM((parts, chunks, LANES), jnp.bfloat16),
            pltpu.VMEM((n, chunks, LANES), jnp.bfloat16),
            pltpu.VMEM((n * chunks, LANES), jnp.float32),
            pltpu.VMEM((n, LANES), jnp.float32),
            pltpu.VMEM((n, 1, LANES), jnp.float32),
            pltpu.VMEM((n, 1, LANES), jnp.float32),
            dma((6,)), dma, dma, dma, dma, dma, dma, dma,
        ],
        compiler_params=pltpu.CompilerParams(
            collective_id=0, has_side_effects=True),
    )(lengths, owner, query_grads, train_factors, basis_in, basis_out, eigenvalues)


def solution(mesh):
    return jax.shard_map(
        local,
        mesh=mesh,
        in_specs=(
            P("dp", None),
            P(("groups", "dp"), None, None),
            P(("groups", "dp")),
            P("groups"),
            P(),
            P(),
            P(),
        ),
        out_specs=P(("groups", "dp"), None),
        check_vma=False,
    )
```

```python
import functools
import math

import jax
import jax.numpy as jnp
from jax import lax
from jax.experimental import pallas as pl
from jax.experimental.pallas import tpu as pltpu
from jax.sharding import PartitionSpec as P

LANES = 128
SUB = 8
NT = (((1,), (1,)), ((), ()))


def nt_dot(a, b, **kw):
    return lax.dot_general(a, b, NT, preferred_element_type=jnp.float32, **kw)


def nn_dot(a, b, **kw):
    return jnp.dot(a, b, preferred_element_type=jnp.float32, **kw)


def iota(shape, dim):
    return lax.broadcasted_iota(jnp.int32, shape, dim)


def each(count, body):
    if count <= 16:
        for step in range(count):
            body(step)
    else:
        lax.fori_loop(0, count, lambda step, c: (body(step), c)[1], 0)


def kernel(n, parts, layers, rank, tokens, q_dev,
           len_hbm, own_hbm, grads_hbm, fact_hbm, bin_hbm, bout_hbm, eig_hbm,
           out_ref,
           len_ref, own_ref, fact, b_in, b_out, eig, bo32, gbuf, hsend, hbuf, wide, score, ssend, sbuf,
           load_sem, gself_sem, gsend_sem, grecv_sem,
           hsend_sem, hrecv_sem, ssend_sem, srecv_sem):
    me = lax.axis_index("dp")
    group = me // parts
    part = me % parts
    width = layers * rank
    feats = layers * rank * rank
    share = feats // parts
    chunks = share // LANES
    per = LANES // rank

    loads = [
        pltpu.make_async_copy(src, dst, load_sem.at[i])
        for i, (src, dst) in enumerate(
            [(bin_hbm, b_in), (bout_hbm, b_out), (eig_hbm, eig), (fact_hbm, fact),
             (len_hbm, len_ref), (own_hbm, own_ref)]
        )
    ]
    for load in loads:
        load.start()
    own_grads = pltpu.make_async_copy(
        grads_hbm.at[:, pl.ds(pl.multiple_of(part * share, share), share)],
        gbuf.at[part], gself_sem)
    own_grads.start()

    barrier = pltpu.get_barrier_semaphore()

    def greet(step):
        peer = (me + step + 1) % n
        pl.semaphore_signal(barrier, inc=1, device_id={"dp": peer},
                            device_id_type=pl.DeviceIdType.MESH)

    each(n - 1, greet)

    for load in loads[:3]:
        load.wait()
    bi = b_in[...].reshape(width, rank)
    bo = b_out[...].reshape(width, rank)
    spread = (iota((rank, width), 0) == iota((rank, width), 1) % rank).astype(jnp.bfloat16)
    spread_t = (iota((width, rank), 0) % rank == iota((width, rank), 1)).astype(jnp.bfloat16)
    lane_layer = iota((width, width), 1) // rank
    same = iota((width, width), 0) // rank == lane_layer
    diag_in32 = jnp.where(same, nn_dot(bi, spread), 0.0)
    diag_in = diag_in32.astype(jnp.bfloat16)
    diag_out_t = jnp.where(same, nt_dot(spread_t, bo), 0.0).astype(jnp.bfloat16)
    rows_in = jnp.sum(diag_in32.reshape(layers, rank, width), axis=0)
    rows_in = jnp.concatenate([rows_in] * per, axis=0).astype(jnp.bfloat16)
    bo32[...] = bo.astype(jnp.float32)
    shuffled = jnp.concatenate(
        [bo32[pl.ds(low, width // per, stride=per), :] for low in range(per)], axis=0
    ).astype(jnp.bfloat16)
    in_order = (iota((width, width), 0) % (width // per)) // (rank // per) == lane_layer
    diag_out = jnp.where(in_order, nn_dot(shuffled, spread), 0.0).astype(jnp.bfloat16)
    values = eig[...]
    damp = 0.1 * (jnp.sum(values, axis=(1, 2), keepdims=True) * (1.0 / (rank * rank)))
    weight = (1.0 / (values + damp)).reshape(width, rank)
    weight = nn_dot(weight, spread.astype(jnp.float32), precision=lax.Precision.HIGHEST)
    weight = jnp.where(same, weight, 0.0)

    for load in loads[3:]:
        load.wait()
    rot_in = nn_dot(fact[0, :, :width], diag_in).astype(jnp.bfloat16)
    rot_out = nt_dot(diag_out_t, fact[0, :, width:])
    live = iota((width, tokens), 1) < len_ref[0]
    rot_out = jnp.where(live, rot_out, 0.0).astype(jnp.bfloat16)
    gram = nn_dot(rot_out, rot_in)
    scaled = (gram * weight).astype(jnp.bfloat16)
    back = nt_dot(scaled, rows_in).astype(jnp.bfloat16)
    back = nn_dot(diag_out, back)
    rows = width // per
    slot = iota((rows, LANES), 1) // rank
    total = jnp.zeros((rows, LANES), jnp.float32)
    for low in range(per):
        total = jnp.where(slot == low, back[low * rows:(low + 1) * rows], total)
    hsend[...] = total.reshape(parts, chunks, LANES).astype(jnp.bfloat16)

    pl.semaphore_wait(barrier, n - 1)

    def send_rows(step):
        peer = (me + step + 1) % n
        pltpu.make_async_remote_copy(
            hsend.at[peer % parts], hbuf.at[me],
            hsend_sem, hrecv_sem, device_id={"dp": peer},
            device_id_type=pl.DeviceIdType.MESH).start()

    each(n - 1, send_rows)
    hbuf[me] = hsend[part]

    def send_grads(step):
        other = (part + step + 1) % parts
        pltpu.make_async_remote_copy(
            grads_hbm.at[:, pl.ds(pl.multiple_of(other * share, share), share)],
            gbuf.at[part], gsend_sem, grecv_sem,
            device_id={"dp": group * parts + other},
            device_id_type=pl.DeviceIdType.MESH).start()

    each(parts - 1, send_grads)

    own_grads.wait()
    some = gbuf.at[pl.ds(0, parts - 1)]
    pltpu.make_async_copy(some, some, grecv_sem).wait()
    grads = gbuf[...].astype(jnp.float32).reshape(parts * q_dev, share).astype(jnp.bfloat16)
    grads = jnp.concatenate([grads] * (LANES // (parts * q_dev)), axis=0)
    others = hbuf.at[pl.ds(0, n - 1)]
    pltpu.make_async_copy(others, others, hrecv_sem).wait()
    wide[...] = hbuf[...].astype(jnp.float32).reshape(n * chunks, LANES)
    sums = jnp.concatenate(
        [wide[pl.ds(c, n, stride=chunks), :].astype(jnp.bfloat16) for c in range(chunks)], axis=1)
    score[...] = nt_dot(sums, grads)

    def order(step):
        ssend[step] = score[pl.ds(own_ref[step], 1), :]

    each(n, order)

    def send_score(step):
        peer = (me + step + 1) % n
        pltpu.make_async_remote_copy(
            ssend.at[peer], sbuf.at[me], ssend_sem, srecv_sem, device_id={"dp": peer},
            device_id_type=pl.DeviceIdType.MESH).start()

    each(n - 1, send_score)
    sbuf[me] = ssend[me]
    rest = sbuf.at[pl.ds(0, n - 1)]
    pltpu.make_async_copy(rest, rest, srecv_sem).wait()

    scale = 1.0 / (rank * math.sqrt(tokens))
    span = parts * q_dev
    lane = iota((1, LANES), 1) // span
    per_block = LANES // span
    for block in range(n // parts // per_block):
        row = jnp.zeros((1, LANES), jnp.float32)
        for at in range(per_block):
            low = (block * per_block + at) * parts
            row = jnp.where(lane == at, jnp.sum(sbuf[low:low + parts], axis=0), row)
        out_ref[:, block * LANES:(block + 1) * LANES] = row * scale

    pltpu.make_async_copy(some, some, gsend_sem).wait()
    pltpu.make_async_copy(others, others, hsend_sem).wait()
    pltpu.make_async_copy(rest, rest, ssend_sem).wait()


def local(query_grads, train_factors, lengths, owner, basis_in, basis_out, eigenvalues):
    layers, rank = (eigenvalues.shape[0], eigenvalues.shape[1])
    n = lax.axis_size("dp")
    seqs, tokens, cols = train_factors.shape
    q_dev, feats = query_grads.shape
    parts = feats // (SUB * LANES)
    share = feats // parts
    width = layers * rank
    chunks = share // LANES
    hbm = pl.BlockSpec(memory_space=pltpu.HBM)
    dma = pltpu.SemaphoreType.DMA
    return pl.pallas_call(
        functools.partial(kernel, n, parts, layers, rank, tokens, q_dev),
        out_shape=jax.ShapeDtypeStruct((1, n * q_dev), jnp.float32),
        in_specs=[hbm] * 7,
        out_specs=pl.BlockSpec(memory_space=pltpu.VMEM),
        scratch_shapes=[
            pltpu.SMEM(lengths.shape, jnp.int32),
            pltpu.SMEM(owner.shape, jnp.int32),
            pltpu.VMEM((seqs, tokens, cols), jnp.bfloat16),
            pltpu.VMEM((layers, rank, rank), jnp.bfloat16),
            pltpu.VMEM((layers, rank, rank), jnp.bfloat16),
            pltpu.VMEM((layers, rank, rank), jnp.float32),
            pltpu.VMEM((width, rank), jnp.float32),
            pltpu.VMEM((parts, q_dev, share), jnp.bfloat16),
            pltpu.VMEM((parts, chunks, LANES), jnp.bfloat16),
            pltpu.VMEM((n, chunks, LANES), jnp.bfloat16),
            pltpu.VMEM((n * chunks, LANES), jnp.float32),
            pltpu.VMEM((n, LANES), jnp.float32),
            pltpu.VMEM((n, 1, LANES), jnp.float32),
            pltpu.VMEM((n, 1, LANES), jnp.float32),
            dma((6,)), dma, dma, dma, dma, dma, dma, dma,
        ],
        compiler_params=pltpu.CompilerParams(
            collective_id=0, has_side_effects=True, vmem_limit_bytes=55226 * 1024),
    )(lengths, owner, query_grads, train_factors, basis_in, basis_out, eigenvalues)


def solution(mesh):
    return jax.shard_map(
        local,
        mesh=mesh,
        in_specs=(
            P("dp", None),
            P(("groups", "dp"), None, None),
            P(("groups", "dp")),
            P("groups"),
            P(),
            P(),
            P(),
        ),
        out_specs=P(("groups", "dp"), None),
        check_vma=False,
    )
```

```python
import functools
import math

import jax
import jax.numpy as jnp
from jax import lax
from jax.experimental import pallas as pl
from jax.experimental.pallas import tpu as pltpu
from jax.sharding import PartitionSpec as P

LANES = 128
SUB = 8
NT = (((1,), (1,)), ((), ()))


def nt_dot(a, b, **kw):
    return lax.dot_general(a, b, NT, preferred_element_type=jnp.float32, **kw)


def nn_dot(a, b, **kw):
    return jnp.dot(a, b, preferred_element_type=jnp.float32, **kw)


def iota(shape, dim):
    return lax.broadcasted_iota(jnp.int32, shape, dim)


def each(count, body):
    if count <= 16:
        for step in range(count):
            body(step)
    else:
        lax.fori_loop(0, count, lambda step, c: (body(step), c)[1], 0)


def kernel(n, parts, layers, rank, tokens, q_dev,
           len_hbm, own_hbm, grads_hbm, fact_hbm, bin_hbm, bout_hbm, eig_hbm,
           out_ref,
           mine, len_ref, own_ref, fact, b_in, b_out, eig, bo32, gbuf, hsend, hbuf, wide, score, ssend, sbuf,
           load_sem, gself_sem, gsend_sem, grecv_sem,
           hsend_sem, hrecv_sem, ssend_sem, srecv_sem):
    me = lax.axis_index("dp")
    size = 2 * parts
    block, spot = me // size, me % size
    part = me % parts
    hubs = n // 2
    is_hub = spot // parts == (block + 1) % 2

    def hub_at(which):
        low = which // parts
        return low * size + ((low + 1) % 2) * parts + which % parts

    width = layers * rank
    feats = layers * rank * rank
    share = feats // parts
    chunks = share // LANES
    per = LANES // rank

    loads = [
        pltpu.make_async_copy(src, dst, load_sem.at[i])
        for i, (src, dst) in enumerate(
            [(bin_hbm, b_in), (bout_hbm, b_out), (eig_hbm, eig), (fact_hbm, fact),
             (len_hbm, len_ref), (own_hbm, own_ref), (grads_hbm, mine)]
        )
    ]
    for load in loads:
        load.start()
    barrier = pltpu.get_barrier_semaphore()

    def signal(peer):
        pl.semaphore_signal(barrier, inc=1, device_id={"dp": peer},
                            device_id_type=pl.DeviceIdType.MESH)

    @pl.when(is_hub)
    def _():
        each(n - 1, lambda step: signal((me + step + 1) % n))

    @pl.when(jnp.logical_not(is_hub))
    def _():
        each(hubs, lambda step: signal(hub_at(step)))

    for load in loads[:3]:
        load.wait()
    bi = b_in[...].reshape(width, rank)
    bo = b_out[...].reshape(width, rank)
    spread = (iota((rank, width), 0) == iota((rank, width), 1) % rank).astype(jnp.bfloat16)
    spread_t = (iota((width, rank), 0) % rank == iota((width, rank), 1)).astype(jnp.bfloat16)
    lane_layer = iota((width, width), 1) // rank
    same = iota((width, width), 0) // rank == lane_layer
    diag_in32 = jnp.where(same, nn_dot(bi, spread), 0.0)
    diag_in = diag_in32.astype(jnp.bfloat16)
    diag_out_t = jnp.where(same, nt_dot(spread_t, bo), 0.0).astype(jnp.bfloat16)
    rows_in = jnp.sum(diag_in32.reshape(layers, rank, width), axis=0)
    rows_in = jnp.concatenate([rows_in] * per, axis=0).astype(jnp.bfloat16)
    bo32[...] = bo.astype(jnp.float32)
    shuffled = jnp.concatenate(
        [bo32[pl.ds(low, width // per, stride=per), :] for low in range(per)], axis=0
    ).astype(jnp.bfloat16)
    in_order = (iota((width, width), 0) % (width // per)) // (rank // per) == lane_layer
    diag_out = jnp.where(in_order, nn_dot(shuffled, spread), 0.0).astype(jnp.bfloat16)
    values = eig[...]
    damp = 0.1 * (jnp.sum(values, axis=(1, 2), keepdims=True) * (1.0 / (rank * rank)))
    weight = (1.0 / (values + damp)).reshape(width, rank)
    weight = nn_dot(weight, spread.astype(jnp.float32), precision=lax.Precision.HIGHEST)
    weight = jnp.where(same, weight, 0.0)

    for load in loads[3:]:
        load.wait()
    rot_in = nn_dot(fact[0, :, :width], diag_in).astype(jnp.bfloat16)
    rot_out = nt_dot(diag_out_t, fact[0, :, width:])
    live = iota((width, tokens), 1) < len_ref[0]
    rot_out = jnp.where(live, rot_out, 0.0).astype(jnp.bfloat16)
    gram = nn_dot(rot_out, rot_in)
    scaled = (gram * weight).astype(jnp.bfloat16)
    back = nt_dot(scaled, rows_in).astype(jnp.bfloat16)
    back = nn_dot(diag_out, back)
    rows = width // per
    slot = iota((rows, LANES), 1) // rank
    total = jnp.zeros((rows, LANES), jnp.float32)
    for low in range(per):
        total = jnp.where(slot == low, back[low * rows:(low + 1) * rows], total)
    hsend[...] = total.reshape(parts, chunks, LANES).astype(jnp.bfloat16)

    @pl.when(is_hub)
    def _():
        pl.semaphore_wait(barrier, n - 1)

    @pl.when(jnp.logical_not(is_hub))
    def _():
        pl.semaphore_wait(barrier, hubs)

    def send_rows(step):
        peer = hub_at(step)

        @pl.when(peer != me)
        def _():
            pltpu.make_async_remote_copy(
                hsend.at[step % parts], hbuf.at[me],
                hsend_sem, hrecv_sem, device_id={"dp": peer},
                device_id_type=pl.DeviceIdType.MESH).start()

    each(hubs, send_rows)

    def share_of(which):
        return mine.at[:, pl.ds(which * share, share)]

    for step in range(parts):
        peer = hub_at(block * parts + step)

        @pl.when(peer != me)
        def _():
            pltpu.make_async_remote_copy(
                share_of(step), gbuf.at[spot], gsend_sem, grecv_sem,
                device_id={"dp": peer}, device_id_type=pl.DeviceIdType.MESH).start()

        @pl.when(peer == me)
        def _():
            pltpu.make_async_copy(share_of(step), gbuf.at[spot], gself_sem).start()

    def take(ref, count, sem):
        some = ref.at[pl.ds(0, count)]
        pltpu.make_async_copy(some, some, sem).wait()

    @pl.when(is_hub)
    def _():
        hbuf[me] = hsend[part]
        pltpu.make_async_copy(share_of(0), gbuf.at[spot], gself_sem).wait()
        take(gbuf, size - 1, grecv_sem)
        grads = gbuf[...].astype(jnp.float32).reshape(size * q_dev, share).astype(jnp.bfloat16)
        grads = jnp.concatenate([grads] * (LANES // (size * q_dev)), axis=0)
        take(hbuf, n - 1, hrecv_sem)
        wide[...] = hbuf[...].astype(jnp.float32).reshape(n * chunks, LANES)
        sums = jnp.concatenate(
            [wide[pl.ds(c, n, stride=chunks), :].astype(jnp.bfloat16) for c in range(chunks)],
            axis=1)
        score[...] = nt_dot(sums, grads)

        slot_of_me = block * parts + part

        def send_score(step):
            peer = (me + step + 1) % n
            ssend[peer] = score[pl.ds(own_ref[peer], 1), :]
            pltpu.make_async_remote_copy(
                ssend.at[peer], sbuf.at[slot_of_me], ssend_sem, srecv_sem,
                device_id={"dp": peer}, device_id_type=pl.DeviceIdType.MESH).start()

        each(n - 1, send_score)
        sbuf[slot_of_me] = score[pl.ds(own_ref[me], 1), :]
        take(sbuf, hubs - 1, srecv_sem)

    @pl.when(jnp.logical_not(is_hub))
    def _():
        take(sbuf, hubs, srecv_sem)

    scale = 1.0 / (rank * math.sqrt(tokens))
    span = size * q_dev
    lane = iota((1, LANES), 1) // span
    per_block = LANES // span
    for tile in range(n // size // per_block):
        row = jnp.zeros((1, LANES), jnp.float32)
        for at in range(per_block):
            low = (tile * per_block + at) * parts
            row = jnp.where(lane == at, jnp.sum(sbuf[low:low + parts], axis=0), row)
        out_ref[:, tile * LANES:(tile + 1) * LANES] = row * scale

    @pl.when(is_hub)
    def _():
        take(gbuf, parts - 1, gsend_sem)
        take(hbuf, hubs - 1, hsend_sem)
        take(ssend, n - 1, ssend_sem)

    @pl.when(jnp.logical_not(is_hub))
    def _():
        take(gbuf, parts, gsend_sem)
        take(hbuf, hubs, hsend_sem)


def local(query_grads, train_factors, lengths, owner, basis_in, basis_out, eigenvalues):
    layers, rank = (eigenvalues.shape[0], eigenvalues.shape[1])
    n = lax.axis_size("dp")
    seqs, tokens, cols = train_factors.shape
    q_dev, feats = query_grads.shape
    parts = feats // (2 * SUB * LANES)
    share = feats // parts
    width = layers * rank
    chunks = share // LANES
    hbm = pl.BlockSpec(memory_space=pltpu.HBM)
    dma = pltpu.SemaphoreType.DMA
    return pl.pallas_call(
        functools.partial(kernel, n, parts, layers, rank, tokens, q_dev),
        out_shape=jax.ShapeDtypeStruct((1, n * q_dev), jnp.float32),
        in_specs=[hbm] * 7,
        out_specs=pl.BlockSpec(memory_space=pltpu.VMEM),
        scratch_shapes=[
            pltpu.VMEM(query_grads.shape, jnp.bfloat16),
            pltpu.SMEM(lengths.shape, jnp.int32),
            pltpu.SMEM(owner.shape, jnp.int32),
            pltpu.VMEM((seqs, tokens, cols), jnp.bfloat16),
            pltpu.VMEM((layers, rank, rank), jnp.bfloat16),
            pltpu.VMEM((layers, rank, rank), jnp.bfloat16),
            pltpu.VMEM((layers, rank, rank), jnp.float32),
            pltpu.VMEM((width, rank), jnp.float32),
            pltpu.VMEM((2 * parts, q_dev, share), jnp.bfloat16),
            pltpu.VMEM((parts, chunks, LANES), jnp.bfloat16),
            pltpu.VMEM((n, chunks, LANES), jnp.bfloat16),
            pltpu.VMEM((n * chunks, LANES), jnp.float32),
            pltpu.VMEM((n, LANES), jnp.float32),
            pltpu.VMEM((n, 1, LANES), jnp.float32),
            pltpu.VMEM((n // 2, 1, LANES), jnp.float32),
            dma((7,)), dma, dma, dma, dma, dma, dma, dma,
        ],
        compiler_params=pltpu.CompilerParams(
            collective_id=0, has_side_effects=True, vmem_limit_bytes=55226 * 1024),
    )(lengths, owner, query_grads, train_factors, basis_in, basis_out, eigenvalues)


def solution(mesh):
    return jax.shard_map(
        local,
        mesh=mesh,
        in_specs=(
            P("dp", None),
            P(("groups", "dp"), None, None),
            P(("groups", "dp")),
            P("groups"),
            P(),
            P(),
            P(),
        ),
        out_specs=P(("groups", "dp"), None),
        check_vma=False,
    )
```

```python
import functools
import math

import jax
import jax.numpy as jnp
from jax import lax
from jax.experimental import pallas as pl
from jax.experimental.pallas import tpu as pltpu
from jax.sharding import PartitionSpec as P

LANES = 128
SUB = 8
NT = (((1,), (1,)), ((), ()))


def nt_dot(a, b, **kw):
    return lax.dot_general(a, b, NT, preferred_element_type=jnp.float32, **kw)


def nn_dot(a, b, **kw):
    return jnp.dot(a, b, preferred_element_type=jnp.float32, **kw)


def iota(shape, dim):
    return lax.broadcasted_iota(jnp.int32, shape, dim)


def each(count, body):
    if count <= 16:
        for step in range(count):
            body(step)
    else:
        lax.fori_loop(0, count, lambda step, c: (body(step), c)[1], 0)


def kernel(n, parts, layers, rank, tokens, q_dev,
           len_hbm, own_hbm, grads_hbm, fact_hbm, bin_hbm, bout_hbm, eig_hbm,
           out_ref,
           len_ref, own_ref, fact, b_in, b_out, eig, bo32, gbuf, hsend, hbuf, wide, score, ssend, sbuf,
           load_sem, gself_sem, gsend_sem, grecv_sem,
           hsend_sem, hrecv_sem, ssend_sem, srecv_sem):
    me = lax.axis_index("dp")
    group = me // parts
    part = me % parts
    width = layers * rank
    feats = layers * rank * rank
    share = feats // parts
    chunks = share // LANES
    per = LANES // rank

    loads = [
        pltpu.make_async_copy(src, dst, load_sem.at[i])
        for i, (src, dst) in enumerate(
            [(bin_hbm, b_in), (bout_hbm, b_out), (eig_hbm, eig), (fact_hbm, fact),
             (len_hbm, len_ref), (own_hbm, own_ref)]
        )
    ]
    for load in loads:
        load.start()
    own_grads = pltpu.make_async_copy(
        grads_hbm.at[:, pl.ds(pl.multiple_of(part * share, share), share)],
        gbuf.at[part], gself_sem)
    own_grads.start()

    barrier = pltpu.get_barrier_semaphore()

    def greet(step):
        peer = (me + step + 1) % n
        pl.semaphore_signal(barrier, inc=1, device_id={"dp": peer},
                            device_id_type=pl.DeviceIdType.MESH)

    each(n - 1, greet)

    for load in loads[:3]:
        load.wait()
    bi = b_in[...].reshape(width, rank)
    bo = b_out[...].reshape(width, rank)
    spread = (iota((rank, width), 0) == iota((rank, width), 1) % rank).astype(jnp.bfloat16)
    spread_t = (iota((width, rank), 0) % rank == iota((width, rank), 1)).astype(jnp.bfloat16)
    lane_layer = iota((width, width), 1) // rank
    same = iota((width, width), 0) // rank == lane_layer
    diag_in32 = jnp.where(same, nn_dot(bi, spread), 0.0)
    diag_in = diag_in32.astype(jnp.bfloat16)
    diag_out_t = jnp.where(same, nt_dot(spread_t, bo), 0.0).astype(jnp.bfloat16)
    rows_in = jnp.sum(diag_in32.reshape(layers, rank, width), axis=0)
    rows_in = jnp.concatenate([rows_in] * per, axis=0).astype(jnp.bfloat16)
    bo32[...] = bo.astype(jnp.float32)
    shuffled = jnp.concatenate(
        [bo32[pl.ds(low, width // per, stride=per), :] for low in range(per)], axis=0
    ).astype(jnp.bfloat16)
    in_order = (iota((width, width), 0) % (width // per)) // (rank // per) == lane_layer
    diag_out = jnp.where(in_order, nn_dot(shuffled, spread), 0.0).astype(jnp.bfloat16)
    values = eig[...]
    damp = 0.1 * (jnp.sum(values, axis=(1, 2), keepdims=True) * (1.0 / (rank * rank)))
    weight = (1.0 / (values + damp)).reshape(width, rank)
    weight = nn_dot(weight, spread.astype(jnp.float32), precision=lax.Precision.HIGHEST)
    weight = jnp.where(same, weight, 0.0)

    for load in loads[3:]:
        load.wait()
    rot_in = nn_dot(fact[0, :, :width], diag_in).astype(jnp.bfloat16)
    rot_out = nt_dot(diag_out_t, fact[0, :, width:])
    live = iota((width, tokens), 1) < len_ref[0]
    rot_out = jnp.where(live, rot_out, 0.0).astype(jnp.bfloat16)
    gram = nn_dot(rot_out, rot_in)
    scaled = (gram * weight).astype(jnp.bfloat16)
    back = nt_dot(scaled, rows_in).astype(jnp.bfloat16)
    back = nn_dot(diag_out, back)
    rows = width // per
    slot = iota((rows, LANES), 1) // rank
    total = jnp.zeros((rows, LANES), jnp.float32)
    for low in range(per):
        total = jnp.where(slot == low, back[low * rows:(low + 1) * rows], total)
    hsend[...] = total.reshape(parts, chunks, LANES).astype(jnp.bfloat16)

    pl.semaphore_wait(barrier, n - 1)

    def send_rows(step):
        peer = (me + step + 1) % n
        pltpu.make_async_remote_copy(
            hsend.at[peer % parts], hbuf.at[me],
            hsend_sem, hrecv_sem, device_id={"dp": peer},
            device_id_type=pl.DeviceIdType.MESH).start()

    each(n - 1, send_rows)
    hbuf[me] = hsend[part]

    def send_grads(step):
        other = (part + step + 1) % parts
        pltpu.make_async_remote_copy(
            grads_hbm.at[:, pl.ds(pl.multiple_of(other * share, share), share)],
            gbuf.at[part], gsend_sem, grecv_sem,
            device_id={"dp": group * parts + other},
            device_id_type=pl.DeviceIdType.MESH).start()

    each(parts - 1, send_grads)

    own_grads.wait()
    some = gbuf.at[pl.ds(0, parts - 1)]
    pltpu.make_async_copy(some, some, grecv_sem).wait()
    grads = gbuf[...].astype(jnp.float32).reshape(parts * q_dev, share).astype(jnp.bfloat16)
    grads = jnp.concatenate([grads] * (LANES // (parts * q_dev)), axis=0)
    others = hbuf.at[pl.ds(0, n - 1)]
    pltpu.make_async_copy(others, others, hrecv_sem).wait()
    wide[...] = hbuf[...].astype(jnp.float32).reshape(n * chunks, LANES)
    sums = jnp.concatenate(
        [wide[pl.ds(c, n, stride=chunks), :].astype(jnp.bfloat16) for c in range(chunks)], axis=1)
    score[...] = nt_dot(sums, grads)

    def send_score(step):
        peer = (me + step + 1) % n
        ssend[peer] = score[pl.ds(own_ref[peer], 1), :]
        pltpu.make_async_remote_copy(
            ssend.at[peer], sbuf.at[me], ssend_sem, srecv_sem, device_id={"dp": peer},
            device_id_type=pl.DeviceIdType.MESH).start()

    each(n - 1, send_score)
    ssend[me] = score[pl.ds(own_ref[me], 1), :]
    sbuf[me] = ssend[me]
    rest = sbuf.at[pl.ds(0, n - 1)]
    pltpu.make_async_copy(rest, rest, srecv_sem).wait()

    scale = 1.0 / (rank * math.sqrt(tokens))
    span = parts * q_dev
    lane = iota((1, LANES), 1) // span
    per_block = LANES // span
    for block in range(n // parts // per_block):
        row = jnp.zeros((1, LANES), jnp.float32)
        for at in range(per_block):
            low = (block * per_block + at) * parts
            row = jnp.where(lane == at, jnp.sum(sbuf[low:low + parts], axis=0), row)
        out_ref[:, block * LANES:(block + 1) * LANES] = row * scale

    pltpu.make_async_copy(some, some, gsend_sem).wait()
    pltpu.make_async_copy(others, others, hsend_sem).wait()
    pltpu.make_async_copy(rest, rest, ssend_sem).wait()


def local(query_grads, train_factors, lengths, owner, basis_in, basis_out, eigenvalues):
    layers, rank = (eigenvalues.shape[0], eigenvalues.shape[1])
    n = lax.axis_size("dp")
    seqs, tokens, cols = train_factors.shape
    q_dev, feats = query_grads.shape
    parts = feats // (SUB * LANES)
    share = feats // parts
    width = layers * rank
    chunks = share // LANES
    hbm = pl.BlockSpec(memory_space=pltpu.HBM)
    dma = pltpu.SemaphoreType.DMA
    return pl.pallas_call(
        functools.partial(kernel, n, parts, layers, rank, tokens, q_dev),
        out_shape=jax.ShapeDtypeStruct((1, n * q_dev), jnp.float32),
        in_specs=[hbm] * 7,
        out_specs=pl.BlockSpec(memory_space=pltpu.VMEM),
        scratch_shapes=[
            pltpu.SMEM(lengths.shape, jnp.int32),
            pltpu.SMEM(owner.shape, jnp.int32),
            pltpu.VMEM((seqs, tokens, cols), jnp.bfloat16),
            pltpu.VMEM((layers, rank, rank), jnp.bfloat16),
            pltpu.VMEM((layers, rank, rank), jnp.bfloat16),
            pltpu.VMEM((layers, rank, rank), jnp.float32),
            pltpu.VMEM((width, rank), jnp.float32),
            pltpu.VMEM((parts, q_dev, share), jnp.bfloat16),
            pltpu.VMEM((parts, chunks, LANES), jnp.bfloat16),
            pltpu.VMEM((n, chunks, LANES), jnp.bfloat16),
            pltpu.VMEM((n * chunks, LANES), jnp.float32),
            pltpu.VMEM((n, LANES), jnp.float32),
            pltpu.VMEM((n, 1, LANES), jnp.float32),
            pltpu.VMEM((n, 1, LANES), jnp.float32),
            dma((6,)), dma, dma, dma, dma, dma, dma, dma,
        ],
        compiler_params=pltpu.CompilerParams(
            collective_id=0, has_side_effects=True, vmem_limit_bytes=55226 * 1024),
    )(lengths, owner, query_grads, train_factors, basis_in, basis_out, eigenvalues)


def solution(mesh):
    return jax.shard_map(
        local,
        mesh=mesh,
        in_specs=(
            P("dp", None),
            P(("groups", "dp"), None, None),
            P(("groups", "dp")),
            P("groups"),
            P(),
            P(),
            P(),
        ),
        out_specs=P(("groups", "dp"), None),
        check_vma=False,
    )
```
